32 devices in a mesh: row: 16 (over z, y, core), col: 2 (over x).
Axes of the slice: x: 2, y: 2, z: 4, core: 2. Of those that a mesh axis runs over, the one named last changes fastest.
Arguments:
- weight: float32 [8192, 4096], P('row', 'col'), may hold values from -0.0625 to 0.0625
- grad: bfloat16 [8192, 4096], P('row', 'col'), may hold values from -6 to 6
- left: bfloat16 [8192, 8192], P('row', 'col'), may hold values from -0.25 to 3, as said below
- right: bfloat16 [4096, 4096], P('row', 'col'), may hold values from -0.25 to 3, as said below
- tokens: bfloat16 [2048, 8192], P('row'), may hold values from -6 to 6
Outputs:
- new_weight: float32 [8192, 4096], P('row', 'col')
- output: bfloat16 [2048, 4096], P('row', 'col')
The draws below stay inside these ranges and needn't reach their ends.
Inputs may be any that keep to these rules, and one draw needn't show every extreme that they name: left is symmetric. right is symmetric.
All inputs are finite; a program needn't handle non-finite values.
Results may differ from the reference program's by a relative error of at most 0.0056.
Values may be sent and summed in bfloat16 or wider, within the bound.
No kernel may reach another device: no remote copies, remote signals or barrier semaphores. Data moves between devices by JAX's collectives and lax.ppermute only.
A program may use at most 128 MiB of HBM per device.

```python
import math
import jax
import jax.numpy as jnp

D = 8192
BLK = 4096
TOKENS = 2048


def symmetric_factor(key, order):
    first_key, second_key = jax.random.split(jax.random.fold_in(key, 7))
    diagonal = jax.random.uniform(first_key, (order,), jnp.float32, 0.5, 2.0)
    scale_off = 0.6 / math.sqrt(order)
    noise = jax.random.uniform(second_key, (order, order), jnp.float32, -1.0, 1.0)
    offdiag = (noise + noise.T) * scale_off
    eye_mask = jnp.eye(order, dtype=jnp.float32)
    offdiag = offdiag * (1.0 - eye_mask)
    return (offdiag + eye_mask * diagonal[:, None]).astype(jnp.bfloat16)


def draw_left(key, part):
    return symmetric_factor(key, D)


def draw_right(key, part):
    return symmetric_factor(jax.random.fold_in(key, 11), BLK)


def levels(rng, shape, shards, least, top_value):
    def one(dim, shards_of):
        draws = jax.random.uniform(jax.random.fold_in(jax.random.fold_in(rng, 6), dim), (shards_of,), jnp.float32, least / len(shards), top_value / len(shards))
        return jnp.repeat(jnp.exp(draws), shape[dim] // shards_of).reshape((-1,) + (1,) * (len(shape) - dim - 1))

    factor_of = one(*shards[0])
    for cut in shards[1:]:
        factor_of = factor_of * one(*cut)
    return factor_of


def centred(own_key, dims, scale, reach, cuts=(), held_as=jnp.bfloat16):
    array = scale * jax.random.normal(own_key, dims, jnp.float32)
    if cuts:
        array = array * levels(own_key, dims, cuts, -0.22, 0.18)
    return jnp.clip(array, -reach, reach).astype(held_as)


def setup_inputs(seed: int = 0) -> dict:
    seeds = jax.random.split(jax.random.key(seed), 6)
    return {
        "weight": centred(seeds[0], (D, BLK), D ** -0.5, 0.0625, ((0, 16), (1, 2)), jnp.float32),
        "grad": centred(seeds[1], (D, BLK), 1.0, 6.0, ((0, 16), (1, 2))),
        "left": draw_left(jax.random.fold_in(seeds[5], 71), 0),
        "right": draw_right(jax.random.fold_in(seeds[5], 71), 0),
        "tokens": centred(seeds[4], (TOKENS, D), 1.0, 6.0, ((0, 16),)),
    }


def reference(weight, grad, left, right, tokens):
    left_grad = jnp.dot(left, grad, preferred_element_type=jnp.float32).astype(jnp.bfloat16)
    precond = jnp.dot(left_grad, right, preferred_element_type=jnp.float32)
    new_weight = weight - 0.01 * precond
    narrow = new_weight.astype(jnp.bfloat16)
    output = jnp.dot(tokens, narrow, preferred_element_type=jnp.float32).astype(jnp.bfloat16)
    return new_weight, output
```

```python
import jax
import jax.numpy as jnp
from jax import lax
from jax.experimental import pallas as pl
from jax.sharding import Mesh, PartitionSpec as P

F32 = jnp.float32
BF16 = jnp.bfloat16
ROWS = ("z", "y", "k")
EIGHTHS = (2, 2, 3, 1)


def shift(block, axis, size, by):
    return lax.ppermute(block, axis, [(i, (i + by) % size) for i in range(size)])


def swap(block, axis):
    return shift(block, axis, 2, 1)


def others(own, axis, size):
    return [shift(own, axis, size, -by) for by in range(1, size)]


def dot(a, b):
    return jnp.dot(a, b, preferred_element_type=F32)


def columns(array, start, width):
    return lax.dynamic_slice_in_dim(array, start, width, 1)


def tie(tree):
    arrays, form = jax.tree.flatten(tree)
    tied = pl.pallas_call(
        lambda *refs: None,
        out_shape=[jax.ShapeDtypeStruct(a.shape, a.dtype) for a in arrays],
        in_specs=[pl.BlockSpec(memory_space=pl.ANY)] * len(arrays),
        out_specs=[pl.BlockSpec(memory_space=pl.ANY)] * len(arrays),
        input_output_aliases={i: i for i in range(len(arrays))},
    )(*arrays)
    return jax.tree.unflatten(form, tied)


def lay(blocks, me, axis):
    n = len(blocks)
    if n == 2:
        a, b = blocks
        first, last = jnp.where(me == 0, a, b), jnp.where(me == 0, b, a)
        return jnp.concatenate([first, last], axis=axis)
    shape = list(blocks[0].shape)
    width, shape[axis] = shape[axis], shape[axis] * n
    whole = jnp.zeros(shape, blocks[0].dtype)
    for by, block in enumerate(blocks):
        whole = lax.dynamic_update_slice_in_dim(whole, block, (me + by) % n * width, axis)
    return whole


def chunks(width):
    parts = EIGHTHS if width % 1024 == 0 else (2, 2, 2, 2)
    ends = [sum(parts[:i]) * width // 8 for i in range(len(parts) + 1)]
    return list(zip(ends, ends[1:]))


def step(sizes, weight, grad, left, right, tokens):
    nz, nx = sizes["z"], sizes["x"]
    y, k, x, z = (lax.axis_index(a) for a in ("y", "k", "x", "z"))
    rows, width = grad.shape
    deep = right.shape[0]
    count = tokens.shape[0]
    part = count // nx
    per = nz // nx
    spans = chunks(width)

    def of_y(array, which, size):
        size *= 2
        return jnp.concatenate(
            [columns(array, (2 * i + which) * size, size) for i in range(per)], axis=1
        )

    share = lax.dynamic_slice_in_dim(tokens, x * part, part, 0)

    def piece(level):
        return jnp.concatenate(
            [
                columns(share, (level * 4 + (y ^ dy) * 2 + (k ^ dk)) * rows, rows)
                for dk in range(2)
                for dy in range(2)
            ],
            axis=1,
        )

    def gather_levels(block):
        return lax.all_gather(block, ("z", "k"), axis=0, tiled=True)

    def multiply_tokens(narrow, near):
        narrow = jnp.concatenate([narrow, near], axis=0)
        narrow = jnp.concatenate([narrow, swap(narrow, "k")], axis=0)
        sums = dot(token_panel, narrow)
        total = sums[:count]
        for by in range(1, nz):
            send = sums[by * count : (by + 1) * count].astype(BF16)
            total += shift(send, "z", nz, -by).astype(F32)
        return total.astype(BF16)

    half = width // 2
    right_panels = [gather_levels(right[:, :half])]
    grad_mine = of_y(grad, y, deep)
    spread = [piece((z + by) % nz) for by in range(nz)]
    now = tie(
        {
            "mine": grad_mine,
            "mine_x": others(grad_mine, "x", nx),
            "borrowed": swap(of_y(grad, 1 - y, deep), "y"),
            "right": right[:, half:],
            "left": [of_y(left, y, rows), of_y(left, 1 - y, rows)],
            "spread": [spread[0]]
            + [shift(spread[by], "z", nz, by) for by in range(1, nz)],
        }
    )
    right_panels.append(gather_levels(now["right"]))
    left_mine, left_lent = now["left"]
    left_mine_x = others(left_mine, "x", nx)
    left_borrowed = swap(left_lent, "y")
    grad_mine = lay([now["mine"], *now["mine_x"]], x, 1)
    grad_borrowed = lay([now["borrowed"], *others(now["borrowed"], "x", nx)], x, 1)
    spread = jnp.concatenate(now["spread"], axis=0)

    def multiply(start, stop):
        which = start // half
        panel = right_panels[which][:, start - which * half : stop - which * half]
        received = swap(dot(grad_borrowed, panel).astype(BF16), "y")
        own = dot(grad_mine, panel) + received.astype(F32)
        return own.astype(BF16)

    product = multiply(*spans[0])
    now = tie(
        {
            "product": product,
            "grad": grad_borrowed,
            "mine_x": left_mine_x,
            "mine": left_mine,
            "borrowed": left_borrowed,
            "spread": spread,
        }
    )
    grad_borrowed = now["grad"]
    products = [now["product"]] + [multiply(*span) for span in spans[1:]]
    left_mine = lay([now["mine"], *now["mine_x"]], x, 1)
    left_borrowed = lay([now["borrowed"], *others(now["borrowed"], "x", nx)], x, 1)
    spread = now["spread"]
    token_panel = lay(
        [b.reshape(nz, part, 4 * rows) for b in [spread, *others(spread, "x", nx)]], x, 1
    ).reshape(nz * count, 4 * rows)

    new_weight, outputs = weight, []
    near = None
    for (start, stop), product in zip(spans, products):
        panel = gather_levels(product)
        if near is not None:
            panel, near = tie((panel, near))
            outputs.append(multiply_tokens(narrow, near))
        received = swap(dot(left_borrowed, panel).astype(BF16), "y")
        precond = dot(left_mine, panel) + received.astype(F32)
        update = weight[:, start:stop] - 0.01 * precond
        new_weight = lax.dynamic_update_slice(new_weight, update, (0, start))
        narrow = update.astype(BF16)
        near = swap(narrow, "y")
    outputs.append(multiply_tokens(narrow, near))
    return new_weight, jnp.concatenate(outputs, axis=1)


def solution(mesh):
    nrow, ncol = mesh.shape["row"], mesh.shape["col"]
    sizes = {"z": nrow // 4, "y": 2, "k": 2, "x": ncol}
    fine = Mesh(mesh.devices.reshape(nrow // 4, 2, 2, ncol), ("z", "y", "k", "x"))
    split = P(ROWS, "x")
    return jax.shard_map(
        lambda *args: step(sizes, *args),
        mesh=fine,
        in_specs=(split, split, split, split, P(ROWS, None)),
        out_specs=(split, split),
        check_vma=False,
    )
```

```python
import jax
import jax.numpy as jnp
from jax import lax
from jax.experimental import pallas as pl
from jax.sharding import Mesh, PartitionSpec as P

F32 = jnp.float32
BF16 = jnp.bfloat16
ROWS = ("z", "y", "k")
SIXTEENTHS = (4, 4, 5, 3)


def shift(block, axis, size, by):
    return lax.ppermute(block, axis, [(i, (i + by) % size) for i in range(size)])


def swap(block, axis):
    return shift(block, axis, 2, 1)


def others(own, axis, size):
    return [shift(own, axis, size, -by) for by in range(1, size)]


def dot(a, b):
    return jnp.dot(a, b, preferred_element_type=F32)


def columns(array, start, width):
    return lax.dynamic_slice_in_dim(array, start, width, 1)


def tie(tree):
    arrays, form = jax.tree.flatten(tree)
    tied = pl.pallas_call(
        lambda *refs: None,
        out_shape=[jax.ShapeDtypeStruct(a.shape, a.dtype) for a in arrays],
        in_specs=[pl.BlockSpec(memory_space=pl.ANY)] * len(arrays),
        out_specs=[pl.BlockSpec(memory_space=pl.ANY)] * len(arrays),
        input_output_aliases={i: i for i in range(len(arrays))},
    )(*arrays)
    return jax.tree.unflatten(form, tied)


def place(whole, blocks, me, row):
    width = blocks[0].shape[1]
    for by, block in enumerate(blocks):
        column = (me + by) % len(blocks) * width
        whole = lax.dynamic_update_slice(whole, block, (row, column))
    return whole


def chunks(width):
    parts = SIXTEENTHS if width % 2048 == 0 else (8, 8)
    ends = [sum(parts[:i]) * width // 16 for i in range(len(parts) + 1)]
    return list(zip(ends, ends[1:]))


def step(sizes, weight, grad, left, right, tokens):
    nz, nx = sizes["z"], sizes["x"]
    y, k, x, z = (lax.axis_index(a) for a in ("y", "k", "x", "z"))
    rows, width = grad.shape
    deep = right.shape[0]
    count = tokens.shape[0]
    part = count // nx
    per = nz // nx
    spans = chunks(width)

    def of_y(array, which, size):
        size *= 2
        return jnp.concatenate(
            [columns(array, (2 * i + which) * size, size) for i in range(per)], axis=1
        )

    share = lax.dynamic_slice_in_dim(tokens, x * part, part, 0)

    def piece(level):
        return jnp.concatenate(
            [
                columns(share, (level * 4 + (y ^ dy) * 2 + (k ^ dk)) * rows, rows)
                for dk in range(2)
                for dy in range(2)
            ],
            axis=1,
        )

    def gather_levels(block):
        return lax.all_gather(block, ("z", "k"), axis=0, tiled=True)

    def multiply_tokens(narrow, near):
        narrow = jnp.concatenate([narrow, near], axis=0)
        narrow = jnp.concatenate([narrow, swap(narrow, "k")], axis=0)
        sums = dot(token_panel, narrow)
        total = sums[:count]
        for by in range(1, nz):
            send = sums[by * count : (by + 1) * count].astype(BF16)
            total += shift(send, "z", nz, -by).astype(F32)
        return total.astype(BF16)

    half, upper = width // 2, rows // 2

    def multiply(borrowed, panel):
        return swap(dot(borrowed, panel).astype(BF16), "y")

    def cut(product, first):
        return [
            product[:, a - first : b - first]
            for a, b in spans
            if first <= a < first + half
        ]

    right_panel = gather_levels(right[:, :half])
    grad_mine = of_y(grad, y, deep)
    left_mine, left_lent = of_y(left, y, rows), of_y(left, 1 - y, rows)
    now = tie(
        {
            "grad": [grad_mine, *others(grad_mine, "x", nx)],
            "borrowed": swap(of_y(grad, 1 - y, deep), "y"),
            "right": right[:, half:],
            "lent": left_lent[:upper],
            "mine": [left_mine[:upper], left_mine[upper:]],
        }
    )
    mine = now["mine"]
    grad_mine = place(jnp.zeros((rows, nz * 2 * deep), BF16), now["grad"], x, 0)
    next_panel = gather_levels(now["right"])
    now = tie(
        {
            "grad": [now["borrowed"], *others(now["borrowed"], "x", nx)],
            "borrowed": swap(now["lent"], "y"),
            "lent": left_lent[upper:],
            "mine": mine[0],
        }
    )
    borrowed = [now["borrowed"]]
    grad_borrowed = place(jnp.zeros((rows, nz * 2 * deep), BF16), now["grad"], x, 0)
    now = tie(
        {
            "mine": [now["mine"], *others(now["mine"], "x", nx)],
            "received": multiply(grad_borrowed, right_panel),
            "grad": grad_borrowed,
            "lent": now["lent"],
            "next": mine[1],
        }
    )
    both = place(jnp.zeros((2 * rows, nz * 2 * rows), BF16), now["mine"], x, 0)
    grad_borrowed = now["grad"]
    product = (dot(grad_mine, right_panel) + now["received"].astype(F32)).astype(BF16)
    products = cut(product, 0)
    early = len(products)
    now = tie(
        {
            "mine": [now["next"], *others(now["next"], "x", nx)],
            "borrowed": swap(now["lent"], "y"),
            "first": borrowed[0],
            "products": products[1:],
            "spread": [piece((z + by) % nz) for by in range(nz)],
        }
    )
    both = place(both, now["mine"], x, upper)
    products[1:] = now["products"]
    panels = [gather_levels(products[0])]
    borrowed = [now["first"], now["borrowed"]]
    spread = now["spread"]
    now = tie(
        {
            "borrowed": [borrowed[0], *others(borrowed[0], "x", nx)],
            "next": borrowed[1],
            "received": multiply(grad_borrowed, next_panel),
            "spread": spread[:1]
            + [shift(spread[by], "z", nz, by) for by in range(1, nz)],
            "products": products[1:],
        }
    )
    both = place(both, now["borrowed"], x, rows)
    products[1:] = now["products"]
    product = (dot(grad_mine, next_panel) + now["received"].astype(F32)).astype(BF16)
    products += cut(product, half)
    now = tie(
        {
            "borrowed": [now["next"], *others(now["next"], "x", nx)],
            "products": products[early:],
            "spread": now["spread"],
        }
    )
    both = place(both, now["borrowed"], x, rows + upper)
    products[early:] = now["products"]
    spread = jnp.concatenate(now["spread"], axis=0)
    spread = [
        block.reshape(nz, part, 4 * rows) for block in [spread, *others(spread, "x", nx)]
    ]
    token_panel = jnp.zeros((nz, count, 4 * rows), BF16)
    for by, block in enumerate(spread):
        token_panel = lax.dynamic_update_slice(
            token_panel, block, (0, (x + by) % nx * part, 0)
        )
    token_panel = token_panel.reshape(nz * count, 4 * rows)

    def updated(span, precond):
        nonlocal new_weight
        start, stop = span
        update = weight[:, start:stop] - 0.01 * precond
        new_weight = lax.dynamic_update_slice(new_weight, update, (0, start))
        narrow = update.astype(BF16)
        return narrow, swap(narrow, "y")

    new_weight, outputs, previous = weight, [], None
    for i, (span, product) in enumerate(zip(spans, products)):
        panel = gather_levels(product) if i else panels[0]
        if previous is not None:
            panel, previous, outputs = tie((panel, previous, outputs))
            outputs.append(multiply_tokens(*previous))
        received = swap(dot(both[rows:], panel).astype(BF16), "y")
        previous = updated(span, dot(both[:rows], panel) + received.astype(F32))
    previous, outputs = tie((previous, outputs))
    outputs.append(multiply_tokens(*previous))
    return new_weight, jnp.concatenate(outputs, axis=1)


def solution(mesh):
    nrow, ncol = mesh.shape["row"], mesh.shape["col"]
    sizes = {"z": nrow // 4, "y": 2, "k": 2, "x": ncol}
    fine = Mesh(mesh.devices.reshape(nrow // 4, 2, 2, ncol), ("z", "y", "k", "x"))
    split = P(ROWS, "x")
    return jax.shard_map(
        lambda *args: step(sizes, *args),
        mesh=fine,
        in_specs=(split, split, split, split, P(ROWS, None)),
        out_specs=(split, split),
        check_vma=False,
    )
```

```python
import jax
import jax.numpy as jnp
from jax import lax
from jax.experimental import pallas as pl
from jax.sharding import Mesh, PartitionSpec as P

F32 = jnp.float32
BF16 = jnp.bfloat16
ROWS = ("z", "y", "k")
SIXTEENTHS = (4, 4, 5, 3)


def shift(block, axis, size, by):
    return lax.ppermute(block, axis, [(i, (i + by) % size) for i in range(size)])


def swap(block, axis):
    return shift(block, axis, 2, 1)


def others(own, axis, size):
    return [shift(own, axis, size, -by) for by in range(1, size)]


def dot(a, b):
    return jnp.dot(a, b, preferred_element_type=F32)


def columns(array, start, width):
    return lax.dynamic_slice_in_dim(array, start, width, 1)


def tie(tree):
    arrays, form = jax.tree.flatten(tree)
    tied = pl.pallas_call(
        lambda *refs: None,
        out_shape=[jax.ShapeDtypeStruct(a.shape, a.dtype) for a in arrays],
        in_specs=[pl.BlockSpec(memory_space=pl.ANY)] * len(arrays),
        out_specs=[pl.BlockSpec(memory_space=pl.ANY)] * len(arrays),
        input_output_aliases={i: i for i in range(len(arrays))},
    )(*arrays)
    return jax.tree.unflatten(form, tied)


def place(whole, blocks, me, row):
    width = blocks[0].shape[1]
    for by, block in enumerate(blocks):
        column = (me + by) % len(blocks) * width
        whole = lax.dynamic_update_slice(whole, block, (row, column))
    return whole


def chunks(width):
    parts = SIXTEENTHS if width % 2048 == 0 else (8, 8)
    ends = [sum(parts[:i]) * width // 16 for i in range(len(parts) + 1)]
    return list(zip(ends, ends[1:]))


def step(sizes, weight, grad, left, right, tokens):
    nz, nx = sizes["z"], sizes["x"]
    y, k, x, z = (lax.axis_index(a) for a in ("y", "k", "x", "z"))
    rows, width = grad.shape
    deep = right.shape[0]
    count = tokens.shape[0]
    part = count // nx
    per = nz // nx
    spans = chunks(width)

    def of_y(array, which, size):
        size *= 2
        return jnp.concatenate(
            [columns(array, (2 * i + which) * size, size) for i in range(per)], axis=1
        )

    share = lax.dynamic_slice_in_dim(tokens, x * part, part, 0)

    def piece(level):
        return jnp.concatenate(
            [
                columns(share, (level * 4 + (y ^ dy) * 2 + (k ^ dk)) * rows, rows)
                for dk in range(2)
                for dy in range(2)
            ],
            axis=1,
        )

    def gather_levels(block):
        return lax.all_gather(block, ("z", "k"), axis=0, tiled=True)

    def multiply_tokens(narrow, near):
        narrow = jnp.concatenate([narrow, near], axis=0)
        narrow = jnp.concatenate([narrow, swap(narrow, "k")], axis=0)
        sums = dot(token_panel, narrow)
        total = sums[:count]
        for by in range(1, nz):
            send = sums[by * count : (by + 1) * count].astype(BF16)
            total += shift(send, "z", nz, -by).astype(F32)
        return total.astype(BF16)

    half, upper = width // 2, rows // 2

    def multiply(borrowed, panel):
        return swap(dot(borrowed, panel).astype(BF16), "y")

    def cut(product, first):
        return [
            product[:, a - first : b - first]
            for a, b in spans
            if first <= a < first + half
        ]

    right_panel = gather_levels(right[:, :half])
    grad_mine = of_y(grad, y, deep)
    left_mine, left_lent = of_y(left, y, rows), of_y(left, 1 - y, rows)
    now = tie(
        {
            "grad": [grad_mine, *others(grad_mine, "x", nx)],
            "borrowed": swap(of_y(grad, 1 - y, deep), "y"),
            "right": right[:, half:],
            "spread": [piece((z + by) % nz) for by in range(nz)],
            "lent": left_lent[:upper],
            "mine": [left_mine[:upper], left_mine[upper:]],
        }
    )
    mine, spread = now["mine"], now["spread"]
    grad_mine = place(jnp.zeros((rows, nz * 2 * deep), BF16), now["grad"], x, 0)
    next_panel = gather_levels(now["right"])
    now = tie(
        {
            "grad": [now["borrowed"], *others(now["borrowed"], "x", nx)],
            "borrowed": swap(now["lent"], "y"),
            "lent": left_lent[upper:],
            "mine": mine[0],
            "spread": spread[:1]
            + [shift(spread[by], "z", nz, by) for by in range(1, nz)],
        }
    )
    borrowed, spread = [now["borrowed"]], now["spread"]
    grad_borrowed = place(jnp.zeros((rows, nz * 2 * deep), BF16), now["grad"], x, 0)
    now = tie(
        {
            "mine": [now["mine"], *others(now["mine"], "x", nx)],
            "received": multiply(grad_borrowed, right_panel),
            "grad": grad_borrowed,
            "lent": now["lent"],
            "next": mine[1],
        }
    )
    both = place(jnp.zeros((2 * rows, nz * 2 * rows), BF16), now["mine"], x, 0)
    grad_borrowed = now["grad"]
    product = (dot(grad_mine, right_panel) + now["received"].astype(F32)).astype(BF16)
    products = cut(product, 0)
    early = len(products)
    now = tie(
        {
            "mine": [now["next"], *others(now["next"], "x", nx)],
            "borrowed": swap(now["lent"], "y"),
            "first": borrowed[0],
            "products": products[1:],
        }
    )
    both = place(both, now["mine"], x, upper)
    products[1:] = now["products"]
    panels = [gather_levels(products[0])]
    borrowed = [now["first"], now["borrowed"]]
    now = tie(
        {
            "borrowed": [borrowed[0], *others(borrowed[0], "x", nx)],
            "next": borrowed[1],
            "received": multiply(grad_borrowed, next_panel),
            "products": products[1:],
        }
    )
    both = place(both, now["borrowed"], x, rows)
    products[1:] = now["products"]
    product = (dot(grad_mine, next_panel) + now["received"].astype(F32)).astype(BF16)
    products += cut(product, half)
    now = tie(
        {
            "borrowed": [now["next"], *others(now["next"], "x", nx)],
            "products": products[early:],
        }
    )
    both = place(both, now["borrowed"], x, rows + upper)
    products[early:] = now["products"]
    spread = jnp.concatenate(spread, axis=0)
    spread = [
        block.reshape(nz, part, 4 * rows) for block in [spread, *others(spread, "x", nx)]
    ]
    token_panel = jnp.zeros((nz, count, 4 * rows), BF16)
    for by, block in enumerate(spread):
        token_panel = lax.dynamic_update_slice(
            token_panel, block, (0, (x + by) % nx * part, 0)
        )
    token_panel = token_panel.reshape(nz * count, 4 * rows)

    def updated(span, precond):
        nonlocal new_weight
        start, stop = span
        update = weight[:, start:stop] - 0.01 * precond
        new_weight = lax.dynamic_update_slice(new_weight, update, (0, start))
        narrow = update.astype(BF16)
        return narrow, swap(narrow, "y")

    new_weight, outputs, previous = weight, [], None
    for i, (span, product) in enumerate(zip(spans, products)):
        panel = gather_levels(product) if i else panels[0]
        if previous is not None:
            panel, previous, outputs = tie((panel, previous, outputs))
            outputs.append(multiply_tokens(*previous))
        received = swap(dot(both[rows:], panel).astype(BF16), "y")
        previous = updated(span, dot(both[:rows], panel) + received.astype(F32))
    previous, outputs = tie((previous, outputs))
    outputs.append(multiply_tokens(*previous))
    return new_weight, jnp.concatenate(outputs, axis=1)


def solution(mesh):
    nrow, ncol = mesh.shape["row"], mesh.shape["col"]
    sizes = {"z": nrow // 4, "y": 2, "k": 2, "x": ncol}
    fine = Mesh(mesh.devices.reshape(nrow // 4, 2, 2, ncol), ("z", "y", "k", "x"))
    split = P(ROWS, "x")
    return jax.shard_map(
        lambda *args: step(sizes, *args),
        mesh=fine,
        in_specs=(split, split, split, split, P(ROWS, None)),
        out_specs=(split, split),
        check_vma=False,
    )
```
